32 devices in a mesh: grp: 2 (over y), tile: 8 (over z, x), corner: 2 (over core).
Axes of the slice: x: 2, y: 2, z: 4, core: 2. Of those that a mesh axis runs over, the one named last changes fastest.
Arguments:
- mask_logits: float32 [768, 512], P(('grp', 'tile'), 'corner'), parts along dimension 0, may hold values from -1.5 to 1.5
- target: bfloat16 [768, 512], P(('grp', 'tile')), parts along dimension 0, may hold values from 0 to 1
- adam_first: float32 [768, 512], P(('grp', 'tile'), 'corner'), parts along dimension 0, may hold values from -1.5 to 1.5
- adam_second: float32 [768, 512], P(('grp', 'tile'), 'corner'), parts along dimension 0, may hold values from 0.05 to 0.2
- tile_counts: int32 [16, 4], P(('grp', 'tile')), parts along dimension 0, may hold values from 0 to 47
- kernels: float32 [2, 8, 2, 35, 35], P('corner'), may hold values from -0.15625 to 0.15625
- socs_weight: float32 [2, 8], P('corner'), may hold values from 0.03 to 0.3
- corner_dose: float32 [2], P('corner'), may hold values from 0.85 to 1.15
Outputs:
- out_logits: float32 [768, 512], P(('grp', 'tile'), 'corner'), parts along dimension 0
- out_first: float32 [768, 512], P(('grp', 'tile'), 'corner'), parts along dimension 0
- out_second: float32 [768, 512], P(('grp', 'tile'), 'corner'), parts along dimension 0
The draws below stay inside these ranges and needn't reach their ends.
There are 2 independent parts, one for each index of `grp`. The reference program is written for one: setup_inputs(seed, part) draws one part's arguments, and reference() takes and returns one part's arrays. A program takes and returns all parts, laid end to end along the dimension named above; an argument that names none is the same for every part. Nothing has to cross between parts.
All inputs are finite; a program needn't handle non-finite values.
Results may differ from the reference program's by a relative error of at most 0.013.
Values may be sent and summed in bfloat16 or wider, within the bound.
A program may use at most 64 MiB of HBM per device.

```python
import math
import jax
import jax.numpy as jnp
from jax import lax

KERN = 8
KS = 35
TILE = 128
TPD = 4
BR = 48
ITERS = 2
HALF = 17
EXT = 82
LR = 88
BC = 512
LC = 640
STRIPS = 8
NR = 384
CORNERS = 2


def plant(result, rng, least, high):
    longest = result.shape.index(max(result.shape))
    spots = []
    for shift in (0, 1):
        where = [jax.random.randint(jax.random.fold_in(rng, axis), (), 0, length) for axis, length in enumerate(result.shape)]
        where[longest] = (where[longest] + shift) % result.shape[longest]
        spots.append(tuple(where))
    return result.at[spots[0]].set(least).at[spots[1]].set(high)


def block_levels(own_key, shape, cuts, low, high):
    def one(axis_at, shards_of):
        steps = jax.random.uniform(jax.random.fold_in(jax.random.fold_in(own_key, 6), axis_at), (shards_of,), jnp.float32, low / len(cuts), high / len(cuts))
        return jnp.repeat(jnp.exp(steps), shape[axis_at] // shards_of).reshape((-1,) + (1,) * (len(shape) - axis_at - 1))

    level = one(*cuts[0])
    for cut in cuts[1:]:
        level = level * one(*cut)
    return level


def centred(stream_key, dims, scale, most, shards=(), kind=jnp.bfloat16):
    drawn = scale * jax.random.normal(stream_key, dims, jnp.float32)
    if shards:
        drawn = drawn * block_levels(stream_key, dims, shards, -0.22, 0.18)
    return jnp.clip(drawn, -most, most).astype(kind)


def setup_inputs(seed: int = 0, part: int = 0) -> dict:
    seeds = jax.random.split(jax.random.key(seed), 9)
    own_keys = jax.random.split(jax.random.fold_in(seeds[8], part), 9)
    return {
        "mask_logits": jnp.clip(jax.random.uniform(own_keys[0], (NR, BC), jnp.float32, -1.5, 1.5) * block_levels(own_keys[0], (NR, BC), ((0, 8), (1, 2)), -0.4, 0.0), -1.5, 1.5),
        "target": jnp.clip(1.0 * jax.random.uniform(own_keys[1], (NR, BC), jnp.float32) ** block_levels(own_keys[1], (NR, BC), ((0, 8),), -0.2, 0.2), 0.0, 1.0).astype(jnp.bfloat16),
        "adam_first": jnp.clip(jax.random.uniform(own_keys[2], (NR, BC), jnp.float32, -1.5, 1.5) * block_levels(own_keys[2], (NR, BC), ((0, 8), (1, 2)), -0.4, 0.0), -1.5, 1.5),
        "adam_second": jnp.clip(jnp.exp(math.log(0.2) - 1.3862944 * jax.random.uniform(own_keys[3], (NR, BC), jnp.float32) ** block_levels(own_keys[3], (NR, BC), ((0, 8), (1, 2)), -0.2, 0.2)), 0.05, 0.2),
        "tile_counts": plant(jax.random.randint(own_keys[4], (STRIPS, TPD), 0, 48), jax.random.fold_in(own_keys[4], 1), 0, 47).astype(jnp.int32),
        "kernels": centred(seeds[5], (CORNERS, KERN, 2, KS, KS), (KS * KS) ** -0.5, 0.15625, ((0, 2),), jnp.float32),
        "socs_weight": jnp.clip(jnp.exp(math.log(0.3) - 2.3025852 * jax.random.uniform(seeds[6], (CORNERS, KERN), jnp.float32) ** block_levels(seeds[6], (CORNERS, KERN), ((0, 2),), -0.2, 0.2)), 0.03, 0.3),
        "corner_dose": jnp.clip(0.85 + 0.29999995 * jax.random.uniform(seeds[7], (CORNERS,), jnp.float32) ** block_levels(seeds[7], (CORNERS,), ((0, 2),), -0.2, 0.2), 0.85, 1.15),
    }


steep = 8.0
thresh = 0.5
loss_scale = 20.0
step_size = 0.05
beta_one = 0.9
beta_two = 0.999
adam_eps = 1e-08
prior_steps = 1000.0

def phase_table(first_index, second_index, length):
    wrapped = jnp.mod(first_index[:, None] * second_index[None, :], length)
    return wrapped.astype(jnp.float32) * (2.0 * math.pi / length)

def dft_tables(strip_rows, kernel_reach, width_all, rows_freq, cols_freq):
    ext_rows = strip_rows + 2 * kernel_reach
    angle_fwd_cols = phase_table(jnp.arange(width_all, dtype=jnp.int32), jnp.arange(cols_freq, dtype=jnp.int32), cols_freq)
    col_fwd = jnp.concatenate([jnp.cos(angle_fwd_cols), -jnp.sin(angle_fwd_cols)], axis=1).astype(jnp.bfloat16)
    angle_fwd_rows = phase_table(jnp.arange(rows_freq, dtype=jnp.int32), jnp.arange(ext_rows, dtype=jnp.int32), rows_freq)
    row_fwd = jnp.concatenate([jnp.cos(angle_fwd_rows), jnp.sin(angle_fwd_rows)], axis=1).astype(jnp.bfloat16)
    angle_inv_rows = phase_table(jnp.arange(strip_rows, dtype=jnp.int32) + kernel_reach, jnp.arange(rows_freq, dtype=jnp.int32), rows_freq)
    row_inv = jnp.concatenate([jnp.cos(angle_inv_rows), jnp.sin(angle_inv_rows)], axis=1).astype(jnp.bfloat16)
    angle_inv_cols = phase_table(jnp.arange(cols_freq, dtype=jnp.int32), jnp.arange(width_all, dtype=jnp.int32), cols_freq)
    cosine_inv = jnp.cos(angle_inv_cols)
    sine_inv = jnp.sin(angle_inv_cols)
    upper_block = jnp.concatenate([cosine_inv, sine_inv], axis=1)
    lower_block = jnp.concatenate([-sine_inv, cosine_inv], axis=1)
    col_inv = jnp.concatenate([upper_block, lower_block], axis=0).astype(jnp.bfloat16)
    return (col_fwd, row_fwd, row_inv, col_inv)

def kernel_spectra(kernels, kernel_reach, rows_freq, cols_freq):
    tap_count = kernels.shape[-1]
    offsets = jnp.arange(tap_count, dtype=jnp.int32) - kernel_reach
    angle_rows = phase_table(jnp.arange(rows_freq, dtype=jnp.int32), offsets, rows_freq)
    angle_cols = phase_table(jnp.arange(cols_freq, dtype=jnp.int32), offsets, cols_freq)
    cosine_rows = jnp.cos(angle_rows)
    sine_rows = jnp.sin(angle_rows)
    cosine_cols = jnp.cos(angle_cols)
    sine_cols = jnp.sin(angle_cols)
    real_taps = kernels[:, :, 0]
    imag_taps = kernels[:, :, 1]
    highest = lax.Precision.HIGHEST

    def contract(form, first_operand, second_operand):
        return jnp.einsum(form, first_operand, second_operand, precision=highest)
    half_real = contract('ckab,gb->ckag', real_taps, cosine_cols) + contract('ckab,gb->ckag', imag_taps, sine_cols)
    half_imag = contract('ckab,gb->ckag', imag_taps, cosine_cols) - contract('ckab,gb->ckag', real_taps, sine_cols)
    spec_real = contract('fa,ckag->ckfg', cosine_rows, half_real) + contract('fa,ckag->ckfg', sine_rows, half_imag)
    spec_imag = contract('fa,ckag->ckfg', cosine_rows, half_imag) - contract('fa,ckag->ckfg', sine_rows, half_real)
    return (spec_real, spec_imag)

def product(form, first_operand, second_operand):
    return jnp.einsum(form, first_operand.astype(jnp.float32), second_operand.astype(jnp.float32), precision=lax.Precision.HIGHEST)

def strip_gradient(mask_ext, target_strip, col_weight, spec_real, spec_imag, socs_weight, corner_dose, tables):
    col_fwd, row_fwd, row_inv, col_inv = tables
    ext_rows = mask_ext.shape[0]
    rows_freq = row_fwd.shape[0]
    cols_freq = col_fwd.shape[1] // 2
    strip_rows = row_inv.shape[0]
    width_all = col_fwd.shape[0]
    corner_count, kernel_count = socs_weight.shape
    normalize = 1.0 / (rows_freq * cols_freq)
    along_cols = jnp.dot(mask_ext, col_fwd, preferred_element_type=jnp.float32).astype(jnp.bfloat16)
    swapped = jnp.concatenate([along_cols[:, cols_freq:], -along_cols[:, :cols_freq]], axis=1)
    stacked = jnp.concatenate([along_cols, swapped], axis=0)
    spectrum = jnp.dot(row_fwd, stacked, preferred_element_type=jnp.float32)
    mask_real = spectrum[:, :cols_freq]
    mask_imag = spectrum[:, cols_freq:]
    prod_real = (mask_real * spec_real - mask_imag * spec_imag).astype(jnp.bfloat16)
    prod_imag = (mask_real * spec_imag + mask_imag * spec_real).astype(jnp.bfloat16)
    blocks = jnp.concatenate([jnp.concatenate([prod_real, prod_imag], axis=3), jnp.concatenate([-prod_imag, prod_real], axis=3)], axis=2)
    row_passed = product('jf,ckfg->ckjg', row_inv, blocks).astype(jnp.bfloat16)
    image_field = jnp.dot(row_passed.reshape(-1, 2 * cols_freq), col_inv, preferred_element_type=jnp.float32)
    image_field = image_field.reshape(corner_count, kernel_count, strip_rows, 2 * width_all) * normalize
    field_real = image_field[..., :width_all]
    field_imag = image_field[..., width_all:]
    weight_wide = socs_weight[:, :, None, None]
    intensity = lax.optimization_barrier(jnp.sum(weight_wide * (field_real * field_real + field_imag * field_imag), axis=1))
    dose_wide = corner_dose[:, None, None]
    resist = jax.nn.sigmoid(steep * (dose_wide * intensity - thresh))
    missed = resist - target_strip.astype(jnp.float32)[None]
    d_int = 2.0 * loss_scale * steep * col_weight[None, None, :] * missed * dose_wide * resist * (1.0 - resist)
    d_amplitude = 2.0 * weight_wide * d_int[:, None]
    d_field = jnp.concatenate([d_amplitude * field_real, d_amplitude * field_imag], axis=3).astype(jnp.bfloat16)
    d_inner = jnp.dot(d_field.reshape(-1, 2 * width_all), col_inv.T, preferred_element_type=jnp.float32) * normalize
    d_inner = d_inner.astype(jnp.bfloat16).reshape(corner_count, kernel_count, strip_rows, 2 * cols_freq)
    d_blocks = product('jf,ckjg->ckfg', row_inv, d_inner)
    upper_part = d_blocks[:, :, :rows_freq]
    lower_part = d_blocks[:, :, rows_freq:]
    d_prod_real = upper_part[..., :cols_freq] + lower_part[..., cols_freq:]
    d_prod_imag = upper_part[..., cols_freq:] - lower_part[..., :cols_freq]
    d_mask_real = lax.optimization_barrier(jnp.sum(d_prod_real * spec_real + d_prod_imag * spec_imag, axis=1))
    d_mask_imag = lax.optimization_barrier(jnp.sum(d_prod_imag * spec_real - d_prod_real * spec_imag, axis=1))
    d_spec = jnp.concatenate([d_mask_real, d_mask_imag], axis=2).astype(jnp.bfloat16)
    d_stacked = product('fj,cfg->cjg', row_fwd, d_spec)
    top_part = d_stacked[:, :ext_rows]
    bottom_part = d_stacked[:, ext_rows:]
    d_along = jnp.concatenate([top_part[..., :cols_freq] - bottom_part[..., cols_freq:], top_part[..., cols_freq:] + bottom_part[..., :cols_freq]], axis=2).astype(jnp.bfloat16)
    return product('cjg,hg->jh', d_along, col_fwd)

def reference(mask_logits, target, adam_first, adam_second, tile_counts, kernels, socs_weight, corner_dose):
    tables = dft_tables(BR, HALF, BC, LR, LC)
    spec_real, spec_imag = kernel_spectra(kernels, HALF, LR, LC)
    counts = tile_counts.astype(jnp.float32)
    col_weights = jnp.repeat(counts / (counts + 4.0), TILE, axis=1)
    target_strips = target.reshape(STRIPS, BR, BC)
    logits = mask_logits
    first = adam_first
    second = adam_second
    for iteration in range(ITERS):
        opacity = jax.nn.sigmoid(logits)
        mask_bf = opacity.astype(jnp.bfloat16)
        padded = jnp.pad(mask_bf, ((HALF, HALF), (0, 0)))

        def one_strip(pieces):
            strip_index, target_strip, col_weight = pieces
            start_row = strip_index * BR
            mask_ext = lax.dynamic_slice_in_dim(padded, start_row, EXT, 0)
            return strip_gradient(mask_ext, target_strip, col_weight, spec_real, spec_imag, socs_weight, corner_dose, tables)
        ext_grads = lax.map(one_strip, (jnp.arange(STRIPS, dtype=jnp.int32), target_strips, col_weights))
        upper_rims = ext_grads[:, :HALF]
        lower_rims = ext_grads[:, HALF + BR:]
        zero_rim = jnp.zeros((1, HALF, BC), jnp.float32)
        from_below = jnp.concatenate([upper_rims[1:], zero_rim], axis=0)
        from_above = jnp.concatenate([zero_rim, lower_rims[:-1]], axis=0)
        grad_mask = ext_grads[:, HALF:HALF + BR]
        grad_mask = grad_mask + jnp.pad(from_below, ((0, 0), (BR - HALF, 0), (0, 0)))
        grad_mask = grad_mask + jnp.pad(from_above, ((0, 0), (0, BR - HALF), (0, 0)))
        gradient = grad_mask.reshape(NR, BC) * opacity * (1.0 - opacity)
        count_now = prior_steps + iteration + 1.0
        first = beta_one * first + (1.0 - beta_one) * gradient
        second = beta_two * second + (1.0 - beta_two) * gradient * gradient
        first_hat = first / (1.0 - beta_one ** count_now)
        second_hat = second / (1.0 - beta_two ** count_now)
        logits = logits - step_size * first_hat / (jnp.sqrt(second_hat) + adam_eps)
    return (logits, first, second)
```

```python
import functools
import math

import jax
import jax.numpy as jnp
import ml_dtypes
import numpy as np
from jax import lax
from jax.experimental import pallas as pl
from jax.experimental.pallas import tpu as pltpu
from jax.sharding import PartitionSpec as P

ITERS = 2

steep = 8.0
thresh = 0.5
loss_scale = 20.0
step_size = 0.05
beta_one = 0.9
beta_two = 0.999
adam_eps = 1e-08
prior_steps = 1000.0

MESH = pl.DeviceIdType.MESH
bf16 = jnp.bfloat16
f32 = jnp.float32


def round_up(count, unit):
    return -(-count // unit) * unit


def tables_of(strip_rows, rim, reach, taps, tap_rows, tap_cols, width, rows_freq, half):
    rows = np.arange(rows_freq)
    omega = 2.0 * np.pi * (np.arange(half) + 0.5) / (2 * half)
    phi = 2.0 * np.pi * rows / rows_freq

    col_angle = np.arange(width)[:, None] * omega[None, :]
    col = np.concatenate([np.cos(col_angle), -np.sin(col_angle)], axis=1)

    place = np.concatenate(
        [
            np.arange(strip_rows) + reach,
            np.arange(rim) - rim + reach,
            np.arange(rim) + reach + strip_rows,
        ]
    )
    used = (place >= 0) & (place < strip_rows + 2 * reach)
    row_angle = phi[:, None] * place[None, :]
    row_cos = np.where(used[None], np.cos(row_angle), 0.0)
    row_sin = np.where(used[None], np.sin(row_angle), 0.0)
    row_fwd = np.concatenate([row_cos, row_sin], axis=1)
    row_fwd_t = np.concatenate([row_cos.T, row_sin.T], axis=1)

    inv_angle = (np.arange(strip_rows)[:, None] + reach) * phi[None, :]
    row_inv = np.concatenate([np.cos(inv_angle), np.sin(inv_angle)], axis=1)
    row_inv_t = np.concatenate([np.cos(inv_angle).T, np.sin(inv_angle).T], axis=1)

    offsets = np.arange(taps) - reach
    tap_col = np.zeros((tap_cols, 2 * half))
    angle = offsets[:, None] * omega[None, :]
    tap_col[:taps, :half] = np.cos(angle)
    tap_col[:taps, half:] = -np.sin(angle)
    tap_row = np.zeros((rows_freq, 2 * tap_rows))
    angle = phi[:, None] * offsets[None, :]
    tap_row[:, :taps] = np.cos(angle)
    tap_row[:, tap_rows : tap_rows + taps] = np.sin(angle)
    found = (col, col.T, row_fwd, row_fwd_t, row_inv, row_inv_t, tap_col, tap_row)
    return [np.ascontiguousarray(table).astype(ml_dtypes.bfloat16) for table in found]


def dot(first, second):
    return jnp.dot(first, second, preferred_element_type=f32)


def kernel_body(
    dims,
    counts_ref,
    weight_ref,
    dose_ref,
    logits_ref,
    target_ref,
    first_ref,
    second_ref,
    taps_ref,
    col_ref,
    col_t_ref,
    row_fwd_ref,
    row_fwd_t_ref,
    row_inv_ref,
    row_inv_t_ref,
    tap_col_ref,
    tap_row_ref,
    out_logits,
    out_first,
    out_second,
    ext,
    grad_out,
    grad_own,
    from_partner,
    from_above,
    from_below,
    tap_pad,
    tap_block,
    spec,
    spectrum,
    ext_block,
    prod_block,
    passed,
    field,
    d_field,
    d_passed,
    d_block,
    d_spec,
    d_spec_block,
    send_sem,
    recv_sem,
):
    strip, rim, reach, taps, tap_rows, width, rows_freq, half, kern, strips, tile_width = dims
    ext_rows = strip + 2 * rim
    planes = 2 * kern
    cols = width // 2
    t = lax.axis_index("tile")
    c = lax.axis_index("corner")
    has_above = t > 0
    has_below = t < strips - 1

    barrier = pltpu.get_barrier_semaphore()

    pl.semaphore_signal(barrier, inc=1, device_id={"corner": 1 - c}, device_id_type=MESH)

    @pl.when(has_above)
    def _():
        for h in range(2):
            pl.semaphore_signal(
                barrier, inc=1, device_id={"tile": t - 1, "corner": h}, device_id_type=MESH
            )

    @pl.when(has_below)
    def _():
        for h in range(2):
            pl.semaphore_signal(
                barrier, inc=1, device_id={"tile": t + 1, "corner": h}, device_id_type=MESH
            )

    @pl.when(jnp.logical_not(has_above))
    def _():
        ext[:, :, strip : strip + rim] = jnp.zeros((ITERS, 2, rim, cols), bf16)

    @pl.when(jnp.logical_not(has_below))
    def _():
        ext[:, :, strip + rim :] = jnp.zeros((ITERS, 2, rim, cols), bf16)

    def remote(src, dst, phase, send_slot, recv_slot, device):
        return pltpu.make_async_remote_copy(
            src_ref=src,
            dst_ref=dst,
            send_sem=send_sem.at[phase, send_slot],
            recv_sem=recv_sem.at[phase, recv_slot],
            device_id=device,
            device_id_type=MESH,
        )

    def mask_copies(it):
        phase = 2 * it
        mine = ext.at[it, c, pl.ds(0, strip)]
        partner = remote(mine, mine, phase, 0, 0, {"corner": 1 - c})
        up = [
            remote(
                ext.at[it, c, pl.ds(0, rim)],
                ext.at[it, c, pl.ds(strip + rim, rim)],
                phase,
                1 + h,
                3 + c,
                {"tile": t - 1, "corner": h},
            )
            for h in range(2)
        ]
        down = [
            remote(
                ext.at[it, c, pl.ds(strip - rim, rim)],
                ext.at[it, c, pl.ds(strip, rim)],
                phase,
                3 + h,
                1 + c,
                {"tile": t + 1, "corner": h},
            )
            for h in range(2)
        ]
        return partner, up, down

    def mask_arrivals(it):
        phase = 2 * it
        partner = ext.at[it, 1 - c, pl.ds(0, strip)]
        partner = remote(partner, partner, phase, 0, 0, {"corner": 1 - c})
        above, below = [], []
        for h in range(2):
            upper = ext.at[it, h, pl.ds(strip, rim)]
            above.append(remote(upper, upper, phase, 0, 1 + h, {"corner": 1 - c}))
            lower = ext.at[it, h, pl.ds(strip + rim, rim)]
            below.append(remote(lower, lower, phase, 0, 3 + h, {"corner": 1 - c}))
        return partner, above, below

    def grad_copies(it):
        phase = 2 * it + 1
        partner = remote(
            grad_out.at[it, 1 - c, pl.ds(0, strip)],
            from_partner.at[it],
            phase,
            0,
            0,
            {"corner": 1 - c},
        )
        up = [
            remote(
                grad_out.at[it, h, pl.ds(strip, rim)],
                from_below.at[it, c],
                phase,
                1 + h,
                3 + c,
                {"tile": t - 1, "corner": h},
            )
            for h in range(2)
        ]
        down = [
            remote(
                grad_out.at[it, h, pl.ds(strip + rim, rim)],
                from_above.at[it, c],
                phase,
                3 + h,
                1 + c,
                {"tile": t + 1, "corner": h},
            )
            for h in range(2)
        ]
        return partner, up, down

    def grad_arrivals(it):
        phase = 2 * it + 1
        land = from_partner.at[it]
        partner = remote(land, land, phase, 0, 0, {"corner": 1 - c})
        above, below = [], []
        for h in range(2):
            upper = from_above.at[it, h]
            above.append(remote(upper, upper, phase, 0, 1 + h, {"corner": 1 - c}))
            lower = from_below.at[it, h]
            below.append(remote(lower, lower, phase, 0, 3 + h, {"corner": 1 - c}))
        return partner, above, below

    def start(copies):
        partner, up, down = copies

        @pl.when(has_above)
        def _():
            for copy in up:
                copy.start()

        @pl.when(has_below)
        def _():
            for copy in down:
                copy.start()

        partner.start()

    def finish_sends(copies):
        partner, up, down = copies
        partner.wait_send()

        @pl.when(has_above)
        def _():
            for copy in up:
                copy.wait_send()

        @pl.when(has_below)
        def _():
            for copy in down:
                copy.wait_send()

    def receive(arrivals):
        partner, above, below = arrivals
        partner.wait_recv()

        @pl.when(has_above)
        def _():
            for copy in above:
                copy.wait_recv()

        @pl.when(has_below)
        def _():
            for copy in below:
                copy.wait_recv()

    opacity = jax.nn.sigmoid(logits_ref[...])
    ext[0, c, 0:strip] = opacity.astype(bf16)
    pl.semaphore_wait(
        barrier, 1 + 2 * has_above.astype(jnp.int32) + 2 * has_below.astype(jnp.int32)
    )
    start(mask_copies(0))

    scale = 2.0 / (rows_freq * 2 * half)
    tap_pad[...] = jnp.zeros(tap_pad.shape, f32)

    def one_spectrum(p, slot):
        tap_pad[slot, 0:taps, 0:taps] = taps_ref[p]
        along = dot(tap_pad[slot].astype(bf16), tap_col_ref[...])
        along_re, along_im = along[:, :half], along[:, half:]
        tap_block[slot, 0:tap_rows, 0:half] = along_re.astype(bf16)
        tap_block[slot, 0:tap_rows, half:] = along_im.astype(bf16)
        tap_block[slot, tap_rows:, 0:half] = along_im.astype(bf16)
        tap_block[slot, tap_rows:, half:] = (-along_re).astype(bf16)
        spec[p] = dot(tap_row_ref[...], tap_block[slot]) * scale

    def spectra_pair(i, _):
        for slot in range(2):
            one_spectrum(2 * i + slot, slot)
        return 0

    lax.fori_loop(0, kern, spectra_pair, 0)

    dose = dose_ref[0]
    weights = []
    for i in range(width // tile_width):
        n = jnp.full((1, tile_width), counts_ref[0, i].astype(f32), f32)
        weights.append(n / (n + 4.0))
    col_weight = jnp.concatenate(weights, axis=1)
    force = 2.0 * loss_scale * steep * dose * col_weight

    for it in range(ITERS):
        receive(mask_arrivals(it))
        along = dot(ext[it, 0], col_ref[0:cols]) + dot(ext[it, 1], col_ref[cols:])
        along_re, along_im = along[:, :half], along[:, half:]
        ext_block[0:ext_rows, 0:half] = along_re.astype(bf16)
        ext_block[0:ext_rows, half:] = along_im.astype(bf16)
        ext_block[ext_rows:, 0:half] = along_im.astype(bf16)
        ext_block[ext_rows:, half:] = (-along_re).astype(bf16)
        spectrum[...] = dot(row_fwd_ref[...], ext_block[...])

        def pass_pair(i, _):
            for slot in range(2):
                p = 2 * i + slot
                s_re, s_im = spectrum[:, 0:half], spectrum[:, half:]
                k_re, k_im = spec[p, :, 0:half], spec[p, :, half:]
                prod_re = s_re * k_re - s_im * k_im
                prod_im = s_re * k_im + s_im * k_re
                prod_block[slot, 0:rows_freq, 0:half] = prod_re.astype(bf16)
                prod_block[slot, 0:rows_freq, half:] = prod_im.astype(bf16)
                prod_block[slot, rows_freq:, 0:half] = (-prod_im).astype(bf16)
                prod_block[slot, rows_freq:, half:] = prod_re.astype(bf16)
                passed[p] = dot(row_inv_ref[...], prod_block[slot]).astype(bf16)
            return 0

        lax.fori_loop(0, kern, pass_pair, 0)

        field[...] = dot(passed[...].reshape(planes * strip, 2 * half), col_t_ref[...]).reshape(
            planes, strip, width
        )
        intensity = jnp.zeros((strip, width), f32)
        for k in range(kern):
            e_re, e_im = field[2 * k], field[2 * k + 1]
            intensity += weight_ref[0, k] * (e_re * e_re + e_im * e_im)
        resist = jax.nn.sigmoid(steep * (dose * intensity - thresh))
        missed = resist - target_ref[...].astype(f32)
        d_int = force * missed * resist * (1.0 - resist)
        for k in range(kern):
            amplitude = (2.0 * weight_ref[0, k]) * d_int
            d_field[2 * k] = (amplitude * field[2 * k]).astype(bf16)
            d_field[2 * k + 1] = (amplitude * field[2 * k + 1]).astype(bf16)
        d_passed[...] = (
            dot(d_field[...].reshape(planes * strip, width), col_ref[...])
            .astype(bf16)
            .reshape(planes, strip, 2 * half)
        )
        d_spec[...] = jnp.zeros(d_spec.shape, f32)

        def back_pair(i, _):
            total_re, total_im = d_spec[:, 0:half], d_spec[:, half:]
            for slot in range(2):
                p = 2 * i + slot
                d_re, d_im = d_passed[p, :, 0:half], d_passed[p, :, half:]
                d_block[slot, 0:strip, 0:half] = d_re
                d_block[slot, 0:strip, half:] = d_im
                d_block[slot, strip:, 0:half] = d_im
                d_block[slot, strip:, half:] = -d_re
                d_prod = dot(row_inv_t_ref[...], d_block[slot])
                p_re, p_im = d_prod[:, :half], d_prod[:, half:]
                k_re, k_im = spec[p, :, 0:half], spec[p, :, half:]
                total_re = total_re + (p_re * k_re + p_im * k_im)
                total_im = total_im + (p_im * k_re - p_re * k_im)
            d_spec[:, 0:half] = total_re
            d_spec[:, half:] = total_im
            return 0

        lax.fori_loop(0, kern, back_pair, 0)

        d_re, d_im = d_spec[:, 0:half], d_spec[:, half:]
        d_spec_block[0:rows_freq, 0:half] = d_re.astype(bf16)
        d_spec_block[0:rows_freq, half:] = d_im.astype(bf16)
        d_spec_block[rows_freq:, 0:half] = (-d_im).astype(bf16)
        d_spec_block[rows_freq:, half:] = d_re.astype(bf16)
        d_along = dot(row_fwd_t_ref[...], d_spec_block[...]).astype(bf16)
        ext_grad = dot(d_along, col_t_ref[...])
        for h in range(2):
            piece = ext_grad[:, h * cols : (h + 1) * cols]
            grad_out[it, h] = piece.astype(bf16)
            grad_own[h] = piece[0:strip]
        start(grad_copies(it))

        logits = logits_ref[...] if it == 0 else out_logits[...]
        first = first_ref[...] if it == 0 else out_first[...]
        second = second_ref[...] if it == 0 else out_second[...]
        opacity = jax.nn.sigmoid(logits)

        @pl.when(jnp.logical_not(has_above))
        def _():
            from_above[it] = jnp.zeros((2, rim, cols), bf16)

        @pl.when(jnp.logical_not(has_below))
        def _():
            from_below[it] = jnp.zeros((2, rim, cols), bf16)

        receive(grad_arrivals(it))
        upper = from_above[it, 0].astype(f32) + from_above[it, 1].astype(f32)
        lower = from_below[it, 0].astype(f32) + from_below[it, 1].astype(f32)
        blank = jnp.zeros((strip - rim, cols), f32)
        grad = grad_own[c] + from_partner[it].astype(f32)
        grad = grad + jnp.concatenate([upper, blank], axis=0)
        grad = grad + jnp.concatenate([blank, lower], axis=0)
        gradient = grad * opacity * (1.0 - opacity)
        count_now = prior_steps + it + 1.0
        first = beta_one * first + (1.0 - beta_one) * gradient
        second = beta_two * second + (1.0 - beta_two) * gradient * gradient
        first_hat = first * (1.0 / (1.0 - beta_one**count_now))
        second_hat = second * (1.0 / (1.0 - beta_two**count_now))
        logits = logits - step_size * first_hat / (jnp.sqrt(second_hat) + adam_eps)
        out_logits[...] = logits
        out_first[...] = first
        out_second[...] = second
        if it + 1 < ITERS:
            ext[it + 1, c, 0:strip] = jax.nn.sigmoid(logits).astype(bf16)
            start(mask_copies(it + 1))
    for it in range(ITERS):
        finish_sends(mask_copies(it))
        finish_sends(grad_copies(it))


def per_device(
    strips,
    mask_logits,
    target,
    adam_first,
    adam_second,
    tile_counts,
    kernels,
    socs_weight,
    corner_dose,
):
    strip, cols = mask_logits.shape
    width = target.shape[1]
    taps = kernels.shape[-1]
    kern = kernels.shape[1]
    reach = taps // 2
    rim = round_up(reach, 16)
    tap_rows = round_up(taps, 16)
    tap_cols = round_up(taps, 128)
    rows_freq = round_up(strip + 2 * reach, 16)
    half = round_up(-(-(width + reach) // 2), 128)
    ext_rows = strip + 2 * rim
    planes = 2 * kern
    tables = tables_of(strip, rim, reach, taps, tap_rows, tap_cols, width, rows_freq, half)
    tile_width = width // tile_counts.shape[1]
    dims = (strip, rim, reach, taps, tap_rows, width, rows_freq, half, kern, strips, tile_width)
    smem = pl.BlockSpec(memory_space=pltpu.SMEM)
    vmem = pl.BlockSpec(memory_space=pltpu.VMEM)
    flops = ITERS * 2 * (2 * planes * strip * 2 * half * (width + 2 * rows_freq))
    return pl.pallas_call(
        functools.partial(kernel_body, dims),
        out_shape=[jax.ShapeDtypeStruct((strip, cols), f32)] * 3,
        in_specs=[smem] * 3 + [vmem] * (5 + len(tables)),
        out_specs=[vmem] * 3,
        scratch_shapes=[
            pltpu.VMEM((ITERS, 2, ext_rows, cols), bf16),
            pltpu.VMEM((ITERS, 2, ext_rows, cols), bf16),
            pltpu.VMEM((2, strip, cols), f32),
            pltpu.VMEM((ITERS, strip, cols), bf16),
            pltpu.VMEM((ITERS, 2, rim, cols), bf16),
            pltpu.VMEM((ITERS, 2, rim, cols), bf16),
            pltpu.VMEM((2, tap_rows, tap_cols), f32),
            pltpu.VMEM((2, 2 * tap_rows, 2 * half), bf16),
            pltpu.VMEM((planes, rows_freq, 2 * half), f32),
            pltpu.VMEM((rows_freq, 2 * half), f32),
            pltpu.VMEM((2 * ext_rows, 2 * half), bf16),
            pltpu.VMEM((2, 2 * rows_freq, 2 * half), bf16),
            pltpu.VMEM((planes, strip, 2 * half), bf16),
            pltpu.VMEM((planes, strip, width), f32),
            pltpu.VMEM((planes, strip, width), bf16),
            pltpu.VMEM((planes, strip, 2 * half), bf16),
            pltpu.VMEM((2, 2 * strip, 2 * half), bf16),
            pltpu.VMEM((rows_freq, 2 * half), f32),
            pltpu.VMEM((2 * rows_freq, 2 * half), bf16),
            pltpu.SemaphoreType.DMA((2 * ITERS, 5)),
            pltpu.SemaphoreType.DMA((2 * ITERS, 5)),
        ],
        compiler_params=pltpu.CompilerParams(
            collective_id=0, has_side_effects=True, vmem_limit_bytes=48 * 1024 * 1024
        ),
        cost_estimate=pl.CostEstimate(flops=flops, bytes_accessed=4 << 20, transcendentals=0),
    )(
        tile_counts,
        socs_weight,
        corner_dose,
        mask_logits,
        target,
        adam_first,
        adam_second,
        kernels.reshape(planes, taps, taps),
        *[jnp.asarray(table) for table in tables],
    )


def solution(mesh):
    pixels = P(("grp", "tile"), "corner")
    rows = P(("grp", "tile"), None)
    return jax.shard_map(
        functools.partial(per_device, mesh.shape["tile"]),
        mesh=mesh,
        in_specs=(
            pixels,
            rows,
            pixels,
            pixels,
            rows,
            P("corner", None, None, None, None),
            P("corner", None),
            P("corner"),
        ),
        out_specs=(pixels, pixels, pixels),
        check_vma=False,
    )
```

```python
import functools
import math

import jax
import jax.numpy as jnp
import ml_dtypes
import numpy as np
from jax import lax
from jax.experimental import pallas as pl
from jax.experimental.pallas import tpu as pltpu
from jax.sharding import PartitionSpec as P

ITERS = 2
TOGETHER = 8
FETCHED = 13

steep = 8.0
thresh = 0.5
loss_scale = 20.0
step_size = 0.05
beta_one = 0.9
beta_two = 0.999
adam_eps = 1e-08
prior_steps = 1000.0

MESH = pl.DeviceIdType.MESH
bf16 = jnp.bfloat16
f32 = jnp.float32


def round_up(count, unit):
    return -(-count // unit) * unit


def tables_of(strip_rows, rim, reach, taps, tap_rows, tap_cols, width, rows_freq, half):
    rows = np.arange(rows_freq)
    omega = 2.0 * np.pi * (np.arange(half) + 0.5) / (2 * half)
    phi = 2.0 * np.pi * rows / rows_freq

    col_angle = np.arange(width)[:, None] * omega[None, :]
    col = np.concatenate([np.cos(col_angle), -np.sin(col_angle)], axis=1)

    place = np.concatenate(
        [
            np.arange(strip_rows) + reach,
            np.arange(rim) - rim + reach,
            np.arange(rim) + reach + strip_rows,
        ]
    )
    used = (place >= 0) & (place < strip_rows + 2 * reach)
    row_angle = phi[:, None] * place[None, :]
    row_cos = np.where(used[None], np.cos(row_angle), 0.0)
    row_sin = np.where(used[None], np.sin(row_angle), 0.0)
    row_fwd = np.concatenate([row_cos, row_sin], axis=1)
    row_fwd_t = np.concatenate([row_cos.T, row_sin.T], axis=1)

    inv_angle = (np.arange(strip_rows)[:, None] + reach) * phi[None, :]
    row_inv = np.concatenate([np.cos(inv_angle), np.sin(inv_angle)], axis=1)
    row_inv_t = np.concatenate([np.cos(inv_angle).T, np.sin(inv_angle).T], axis=1)

    offsets = np.arange(taps) - reach
    tap_col = np.zeros((tap_cols, 2 * half))
    angle = offsets[:, None] * omega[None, :]
    tap_col[:taps, :half] = np.cos(angle)
    tap_col[:taps, half:] = -np.sin(angle)
    tap_row = np.zeros((2 * rows_freq, 2 * tap_rows))
    angle = phi[:, None] * offsets[None, :]
    for part in range(2):
        own = slice(part * rows_freq, (part + 1) * rows_freq)
        tap_row[own, part : 2 * taps : 2] = np.cos(angle)
        tap_row[own, tap_rows + part : tap_rows + 2 * taps : 2] = np.sin(angle)
    found = (col, col.T, row_fwd, row_fwd_t, row_inv, row_inv_t, tap_col, tap_row)
    return [np.ascontiguousarray(table).astype(ml_dtypes.bfloat16) for table in found]


def dot(first, second):
    return jnp.dot(first, second, preferred_element_type=f32)


def adam(it, gradient, logits, first, second):
    count_now = prior_steps + it + 1.0
    first = beta_one * first + (1.0 - beta_one) * gradient
    second = beta_two * second + (1.0 - beta_two) * gradient * gradient
    first_hat = first * (1.0 / (1.0 - beta_one**count_now))
    second_hat = second * (1.0 / (1.0 - beta_two**count_now))
    logits = logits - step_size * first_hat / (jnp.sqrt(second_hat) + adam_eps)
    return logits, first, second


def kernel_body(
    dims,
    counts_ref,
    weight_ref,
    dose_ref,
    *refs,
):
    (strip, rim, reach, taps, tap_rows, width, rows_freq, half, kern, strips, tile_width) = dims
    sources, refs = refs[:FETCHED], refs[FETCHED:]
    outs, refs = refs[:4], refs[4:]
    kept, refs = refs[:FETCHED], refs[FETCHED:]
    out_logits, out_first, out_second, out_gradient = outs
    (
        logits_ref,
        taps_ref,
        tap_col_ref,
        tap_row_ref,
        col_ref,
        row_fwd_ref,
        row_inv_ref,
        col_t_ref,
        target_ref,
        row_inv_t_ref,
        row_fwd_t_ref,
        first_ref,
        second_ref,
    ) = kept
    (
    ext,
    grad_out,
    grad_own,
    from_partner,
    from_above,
    from_below,
    tap_pad,
    tap_block,
    spec,
    spectrum,
    ext_block,
    prod_block,
    passed,
    field,
    d_field,
    d_passed,
    d_block,
    d_spec,
    d_spec_block,
    send_sem,
    recv_sem,
    local_sem,
    ) = refs
    ext_rows = strip + 2 * rim
    planes = 2 * kern
    cols = width // 2
    t = lax.axis_index("tile")
    c = lax.axis_index("corner")
    has_above = t > 0
    has_below = t < strips - 1

    fetches = [
        pltpu.make_async_copy(source, held, local_sem.at[i])
        for i, (source, held) in enumerate(zip(sources, kept))
    ]
    for fetch in fetches:
        fetch.start()

    barrier = pltpu.get_barrier_semaphore()

    pl.semaphore_signal(barrier, inc=1, device_id={"corner": 1 - c}, device_id_type=MESH)

    @pl.when(has_above)
    def _():
        for h in range(2):
            pl.semaphore_signal(
                barrier, inc=1, device_id={"tile": t - 1, "corner": h}, device_id_type=MESH
            )

    @pl.when(has_below)
    def _():
        for h in range(2):
            pl.semaphore_signal(
                barrier, inc=1, device_id={"tile": t + 1, "corner": h}, device_id_type=MESH
            )

    @pl.when(jnp.logical_not(has_above))
    def _():
        ext[:, :, strip : strip + rim] = jnp.zeros((ITERS, 2, rim, cols), bf16)

    @pl.when(jnp.logical_not(has_below))
    def _():
        ext[:, :, strip + rim :] = jnp.zeros((ITERS, 2, rim, cols), bf16)

    def remote(src, dst, phase, send_slot, recv_slot, device):
        return pltpu.make_async_remote_copy(
            src_ref=src,
            dst_ref=dst,
            send_sem=send_sem.at[phase, send_slot],
            recv_sem=recv_sem.at[phase, recv_slot],
            device_id=device,
            device_id_type=MESH,
        )

    def mask_copies(it):
        phase = 2 * it
        mine = ext.at[it, c, pl.ds(0, strip)]
        partner = remote(mine, mine, phase, 0, 0, {"corner": 1 - c})
        up = [
            remote(
                ext.at[it, c, pl.ds(0, rim)],
                ext.at[it, c, pl.ds(strip + rim, rim)],
                phase,
                1 + h,
                3 + c,
                {"tile": t - 1, "corner": h},
            )
            for h in range(2)
        ]
        down = [
            remote(
                ext.at[it, c, pl.ds(strip - rim, rim)],
                ext.at[it, c, pl.ds(strip, rim)],
                phase,
                3 + h,
                1 + c,
                {"tile": t + 1, "corner": h},
            )
            for h in range(2)
        ]
        return partner, up, down

    def mask_arrivals(it):
        phase = 2 * it
        partner = ext.at[it, 1 - c, pl.ds(0, strip)]
        partner = remote(partner, partner, phase, 0, 0, {"corner": 1 - c})
        above, below = [], []
        for h in range(2):
            upper = ext.at[it, h, pl.ds(strip, rim)]
            above.append(remote(upper, upper, phase, 0, 1 + h, {"corner": 1 - c}))
            lower = ext.at[it, h, pl.ds(strip + rim, rim)]
            below.append(remote(lower, lower, phase, 0, 3 + h, {"corner": 1 - c}))
        return partner, above, below

    def grad_copies(it):
        phase = 2 * it + 1
        partner = remote(
            grad_out.at[it, 1 - c, pl.ds(0, strip)],
            from_partner.at[it],
            phase,
            0,
            0,
            {"corner": 1 - c},
        )
        up = [
            remote(
                grad_out.at[it, h, pl.ds(strip, rim)],
                from_below.at[it, c],
                phase,
                1 + h,
                3 + c,
                {"tile": t - 1, "corner": h},
            )
            for h in range(2)
        ]
        down = [
            remote(
                grad_out.at[it, h, pl.ds(strip + rim, rim)],
                from_above.at[it, c],
                phase,
                3 + h,
                1 + c,
                {"tile": t + 1, "corner": h},
            )
            for h in range(2)
        ]
        return partner, up, down

    def grad_arrivals(it):
        phase = 2 * it + 1
        land = from_partner.at[it]
        partner = remote(land, land, phase, 0, 0, {"corner": 1 - c})
        above, below = [], []
        for h in range(2):
            upper = from_above.at[it, h]
            above.append(remote(upper, upper, phase, 0, 1 + h, {"corner": 1 - c}))
            lower = from_below.at[it, h]
            below.append(remote(lower, lower, phase, 0, 3 + h, {"corner": 1 - c}))
        return partner, above, below

    def start(copies):
        partner, up, down = copies

        @pl.when(has_above)
        def _():
            for copy in up:
                copy.start()

        @pl.when(has_below)
        def _():
            for copy in down:
                copy.start()

        partner.start()

    def finish_sends(copies):
        partner, up, down = copies
        partner.wait_send()

        @pl.when(has_above)
        def _():
            for copy in up:
                copy.wait_send()

        @pl.when(has_below)
        def _():
            for copy in down:
                copy.wait_send()

    def receive(arrivals):
        partner, above, below = arrivals
        partner.wait_recv()

        @pl.when(has_above)
        def _():
            for copy in above:
                copy.wait_recv()

        @pl.when(has_below)
        def _():
            for copy in below:
                copy.wait_recv()

    fetches[0].wait()
    opacity = jax.nn.sigmoid(logits_ref[...])
    ext[0, c, 0:strip] = opacity.astype(bf16)
    pl.semaphore_wait(
        barrier, 1 + 2 * has_above.astype(jnp.int32) + 2 * has_below.astype(jnp.int32)
    )
    start(mask_copies(0))

    scale = 2.0 / (rows_freq * 2 * half)
    tap_pad[...] = jnp.zeros(tap_pad.shape, f32)

    def one_spectrum(k, slot):
        tap_pad[slot, 0 : 2 * taps, 0:taps] = taps_ref[k].reshape(2 * taps, taps)
        along = dot(tap_pad[slot].astype(bf16), tap_col_ref[...])
        along_re, along_im = along[:, :half], along[:, half:]
        tap_block[slot, 0:tap_rows, 0:half] = along_re.astype(bf16)
        tap_block[slot, 0:tap_rows, half:] = along_im.astype(bf16)
        tap_block[slot, tap_rows:, 0:half] = along_im.astype(bf16)
        tap_block[slot, tap_rows:, half:] = (-along_re).astype(bf16)
        both = dot(tap_row_ref[...], tap_block[slot]) * scale
        spec[2 * k] = both[0:rows_freq]
        spec[2 * k + 1] = both[rows_freq:]

    def spectra_group(i, _):
        for slot in range(TOGETHER):
            one_spectrum(TOGETHER * i + slot, slot)
        return 0

    for fetch in fetches[1:4]:
        fetch.wait()
    lax.fori_loop(0, kern // TOGETHER, spectra_group, 0)
    for fetch in fetches[4:]:
        fetch.wait()

    dose = dose_ref[0]
    weights = []
    for i in range(width // tile_width):
        n = jnp.full((1, tile_width), counts_ref[0, i].astype(f32), f32)
        weights.append(n / (n + 4.0))
    col_weight = jnp.concatenate(weights, axis=1)
    force = 2.0 * loss_scale * steep * dose * col_weight

    for it in range(ITERS):
        receive(mask_arrivals(it))
        along = dot(ext[it, 0], col_ref[0:cols]) + dot(ext[it, 1], col_ref[cols:])
        along_re, along_im = along[:, :half], along[:, half:]
        ext_block[0:ext_rows, 0:half] = along_re.astype(bf16)
        ext_block[0:ext_rows, half:] = along_im.astype(bf16)
        ext_block[ext_rows:, 0:half] = along_im.astype(bf16)
        ext_block[ext_rows:, half:] = (-along_re).astype(bf16)
        spectrum[...] = dot(row_fwd_ref[...], ext_block[...])

        def pass_group(i, _):
            for slot in range(TOGETHER):
                p = TOGETHER * i + slot
                s_re, s_im = spectrum[:, 0:half], spectrum[:, half:]
                k_re, k_im = spec[p, :, 0:half], spec[p, :, half:]
                prod_re = s_re * k_re - s_im * k_im
                prod_im = s_re * k_im + s_im * k_re
                prod_block[slot, 0:rows_freq, 0:half] = prod_re.astype(bf16)
                prod_block[slot, 0:rows_freq, half:] = prod_im.astype(bf16)
                prod_block[slot, rows_freq:, 0:half] = (-prod_im).astype(bf16)
                prod_block[slot, rows_freq:, half:] = prod_re.astype(bf16)
                passed[p] = dot(row_inv_ref[...], prod_block[slot]).astype(bf16)
            return 0

        lax.fori_loop(0, planes // TOGETHER, pass_group, 0)

        field[...] = dot(passed[...].reshape(planes * strip, 2 * half), col_t_ref[...]).reshape(
            planes, strip, width
        )
        intensity = jnp.zeros((strip, width), f32)
        for k in range(kern):
            e_re, e_im = field[2 * k], field[2 * k + 1]
            intensity += weight_ref[0, k] * (e_re * e_re + e_im * e_im)
        resist = jax.nn.sigmoid(steep * (dose * intensity - thresh))
        missed = resist - target_ref[...].astype(f32)
        d_int = force * missed * resist * (1.0 - resist)
        for k in range(kern):
            amplitude = (2.0 * weight_ref[0, k]) * d_int
            d_field[2 * k] = (amplitude * field[2 * k]).astype(bf16)
            d_field[2 * k + 1] = (amplitude * field[2 * k + 1]).astype(bf16)
        d_passed[...] = (
            dot(d_field[...].reshape(planes * strip, width), col_ref[...])
            .astype(bf16)
            .reshape(planes, strip, 2 * half)
        )
        d_spec[...] = jnp.zeros(d_spec.shape, f32)

        def back_group(i, _):
            total_re, total_im = d_spec[:, 0:half], d_spec[:, half:]
            for slot in range(TOGETHER):
                p = TOGETHER * i + slot
                d_re, d_im = d_passed[p, :, 0:half], d_passed[p, :, half:]
                d_block[slot, 0:strip, 0:half] = d_re
                d_block[slot, 0:strip, half:] = d_im
                d_block[slot, strip:, 0:half] = d_im
                d_block[slot, strip:, half:] = -d_re
                d_prod = dot(row_inv_t_ref[...], d_block[slot])
                p_re, p_im = d_prod[:, :half], d_prod[:, half:]
                k_re, k_im = spec[p, :, 0:half], spec[p, :, half:]
                total_re = total_re + (p_re * k_re + p_im * k_im)
                total_im = total_im + (p_im * k_re - p_re * k_im)
            d_spec[:, 0:half] = total_re
            d_spec[:, half:] = total_im
            return 0

        lax.fori_loop(0, planes // TOGETHER, back_group, 0)

        d_re, d_im = d_spec[:, 0:half], d_spec[:, half:]
        d_spec_block[0:rows_freq, 0:half] = d_re.astype(bf16)
        d_spec_block[0:rows_freq, half:] = d_im.astype(bf16)
        d_spec_block[rows_freq:, 0:half] = (-d_im).astype(bf16)
        d_spec_block[rows_freq:, half:] = d_re.astype(bf16)
        d_along = dot(row_fwd_t_ref[...], d_spec_block[...]).astype(bf16)
        ext_grad = dot(d_along, col_t_ref[...])
        for h in range(2):
            piece = ext_grad[:, h * cols : (h + 1) * cols]
            grad_out[it, h] = piece.astype(bf16)
            grad_own[h] = piece[0:strip]
        start(grad_copies(it))

        logits = logits_ref[...] if it == 0 else out_logits[...]
        first = first_ref[...] if it == 0 else out_first[...]
        second = second_ref[...] if it == 0 else out_second[...]
        opacity = jax.nn.sigmoid(logits)

        @pl.when(jnp.logical_not(has_above))
        def _():
            from_above[it] = jnp.zeros((2, rim, cols), bf16)

        @pl.when(jnp.logical_not(has_below))
        def _():
            from_below[it] = jnp.zeros((2, rim, cols), bf16)

        receive(grad_arrivals(it))
        upper = from_above[it, 0].astype(f32) + from_above[it, 1].astype(f32)
        lower = from_below[it, 0].astype(f32) + from_below[it, 1].astype(f32)
        blank = jnp.zeros((strip - rim, cols), f32)
        grad = grad_own[c] + from_partner[it].astype(f32)
        grad = grad + jnp.concatenate([upper, blank], axis=0)
        grad = grad + jnp.concatenate([blank, lower], axis=0)
        gradient = grad * opacity * (1.0 - opacity)
        if it + 1 < ITERS:
            logits, first, second = adam(it, gradient, logits, first, second)
            ext[it + 1, c, 0:strip] = jax.nn.sigmoid(logits).astype(bf16)
            start(mask_copies(it + 1))
            out_logits[...] = logits
            out_first[...] = first
            out_second[...] = second
        else:
            out_gradient[...] = gradient
    for it in range(ITERS):
        finish_sends(mask_copies(it))
        finish_sends(grad_copies(it))


def per_device(
    strips,
    mask_logits,
    target,
    adam_first,
    adam_second,
    tile_counts,
    kernels,
    socs_weight,
    corner_dose,
):
    strip, cols = mask_logits.shape
    width = target.shape[1]
    taps = kernels.shape[-1]
    kern = kernels.shape[1]
    reach = taps // 2
    rim = round_up(reach, 16)
    tap_rows = round_up(2 * taps, 16)
    tap_cols = round_up(taps, 128)
    rows_freq = round_up(strip + 2 * reach, 16)
    half = round_up(-(-(width + reach) // 2), 128)
    ext_rows = strip + 2 * rim
    planes = 2 * kern
    tables = tables_of(strip, rim, reach, taps, tap_rows, tap_cols, width, rows_freq, half)
    tile_width = width // tile_counts.shape[1]
    dims = (strip, rim, reach, taps, tap_rows, width, rows_freq, half, kern, strips, tile_width)
    smem = pl.BlockSpec(memory_space=pltpu.SMEM)
    vmem = pl.BlockSpec(memory_space=pltpu.VMEM)
    flops = ITERS * 2 * (2 * planes * strip * 2 * half * (width + 2 * rows_freq))
    hbm = pl.BlockSpec(memory_space=pltpu.HBM)
    col, col_t, row_fwd, row_fwd_t, row_inv, row_inv_t, tap_col, tap_row = map(jnp.asarray, tables)
    fetched = (
        mask_logits,
        jnp.swapaxes(kernels[0], 1, 2),
        tap_col,
        tap_row,
        col,
        row_fwd,
        row_inv,
        col_t,
        target,
        row_inv_t,
        row_fwd_t,
        adam_first,
        adam_second,
    )
    logits, first, second, gradient = pl.pallas_call(
        functools.partial(kernel_body, dims),
        out_shape=[jax.ShapeDtypeStruct((strip, cols), f32)] * 4,
        in_specs=[smem] * 3 + [hbm] * len(fetched),
        out_specs=[vmem] * 4,
        scratch_shapes=[
            *[pltpu.VMEM(array.shape, array.dtype) for array in fetched],
            pltpu.VMEM((ITERS, 2, ext_rows, cols), bf16),
            pltpu.VMEM((ITERS, 2, ext_rows, cols), bf16),
            pltpu.VMEM((2, strip, cols), f32),
            pltpu.VMEM((ITERS, strip, cols), bf16),
            pltpu.VMEM((ITERS, 2, rim, cols), bf16),
            pltpu.VMEM((ITERS, 2, rim, cols), bf16),
            pltpu.VMEM((TOGETHER, tap_rows, tap_cols), f32),
            pltpu.VMEM((TOGETHER, 2 * tap_rows, 2 * half), bf16),
            pltpu.VMEM((planes, rows_freq, 2 * half), f32),
            pltpu.VMEM((rows_freq, 2 * half), f32),
            pltpu.VMEM((2 * ext_rows, 2 * half), bf16),
            pltpu.VMEM((TOGETHER, 2 * rows_freq, 2 * half), bf16),
            pltpu.VMEM((planes, strip, 2 * half), bf16),
            pltpu.VMEM((planes, strip, width), f32),
            pltpu.VMEM((planes, strip, width), bf16),
            pltpu.VMEM((planes, strip, 2 * half), bf16),
            pltpu.VMEM((TOGETHER, 2 * strip, 2 * half), bf16),
            pltpu.VMEM((rows_freq, 2 * half), f32),
            pltpu.VMEM((2 * rows_freq, 2 * half), bf16),
            pltpu.SemaphoreType.DMA((2 * ITERS, 5)),
            pltpu.SemaphoreType.DMA((2 * ITERS, 5)),
            pltpu.SemaphoreType.DMA((len(fetched),)),
        ],
        compiler_params=pltpu.CompilerParams(
            collective_id=0, has_side_effects=True, vmem_limit_bytes=60 * 1024 * 1024
        ),
        cost_estimate=pl.CostEstimate(flops=flops, bytes_accessed=4 << 20, transcendentals=0),
    )(
        tile_counts,
        socs_weight,
        corner_dose,
        *fetched,
    )
    return adam(ITERS - 1, gradient, logits, first, second)


def solution(mesh):
    pixels = P(("grp", "tile"), "corner")
    rows = P(("grp", "tile"), None)
    return jax.shard_map(
        functools.partial(per_device, mesh.shape["tile"]),
        mesh=mesh,
        in_specs=(
            pixels,
            rows,
            pixels,
            pixels,
            rows,
            P("corner", None, None, None, None),
            P("corner", None),
            P("corner"),
        ),
        out_specs=(pixels, pixels, pixels),
        check_vma=False,
    )
```
